32 devices in a mesh: groups: 2 (over y), tensor: 4 (over z), dp: 2 (over x), sub: 2 (over core).
Axes of the slice: x: 2, y: 2, z: 4, core: 2. Of those that a mesh axis runs over, the one named last changes fastest.
Arguments:
- output_gradient: bfloat16 [1024, 8192], P(('groups', 'tensor'), ('dp', 'sub')), parts along dimension 0, may hold values from -6 to 6
- hidden_input: bfloat16 [1024, 28672], P(('groups', 'dp', 'sub'), 'tensor'), parts along dimension 0, may hold values from -6 to 6
- frozen_down_matrix: bfloat16 [28672, 8192], P('tensor', ('dp', 'sub')), may hold values from -0.0625 to 0.0625
- down_factors: bfloat16 [16, 16, 28672], P('groups', None, 'tensor'), parts along dimension 0, may hold values from -0.03125 to 0.03125
- up_factors: bfloat16 [16, 16, 8192], P('groups', None, ('dp', 'sub')), parts along dimension 0, may hold values from -0.13183594 to 0.13183594
- token_adapter_index: int32 [1024], P(('groups', 'dp', 'sub')), parts along dimension 0, may hold values from 0 to 7, never falling along the last dimension, each value on 1 to 256 neighbouring positions
Outputs:
- hidden_input_gradient: bfloat16 [1024, 28672], P(('groups', 'dp', 'sub'), 'tensor'), parts along dimension 0
- down_factor_gradient: float32 [16, 16, 28672], P('groups', None, 'tensor'), parts along dimension 0
- up_factor_gradient: float32 [16, 16, 8192], P('groups', None, ('dp', 'sub')), parts along dimension 0
The draws below stay inside these ranges and needn't reach their ends.
There are 2 independent parts, one for each index of `groups`. The reference program is written for one: setup_inputs(seed, part) draws one part's arguments, and reference() takes and returns one part's arrays. A program takes and returns all parts, laid end to end along the dimension named above; an argument that names none is the same for every part. Nothing has to cross between parts.
Inputs may be any that keep to these rules, and one draw needn't show every extreme that they name: `token_adapter_index`: never falls along the tokens; each adapter has 1 to 256 tokens and some adapter has exactly 256.
All inputs are finite; a program needn't handle non-finite values.
Results may differ from the reference program's by a relative error of at most 0.014.
Values may be sent and summed in bfloat16 or wider, within the bound.
A program may use at most 128 MiB of HBM per device.

```python
import math
import jax
import jax.numpy as jnp
import numpy as np
from jax import lax

OUTPUT_FEATURES = 8192
HIDDEN_UNITS = 28672
ADAPTER_RANK = 16
ADAPTER_SLOTS = 8
SHARD_TOKENS = 128
TOKENS = 512
N_DP = 2
N_SUB = 2


def spiked(entries, own_key, source, target, shards_of, factor):
    def block_of(dim):
        return (jnp.arange(entries.shape[dim]) // (entries.shape[dim] // shards_of)).reshape((-1,) + (1,) * (entries.ndim - 1 - dim))

    first = jax.random.permutation(own_key, shards_of)[block_of(target)]
    other_side = (block_of(target) + shards_of // 2) % shards_of
    return jnp.where((block_of(source) == first) | (block_of(source) == other_side), factor * entries, entries)


def steps_of(key, extent, cuts, smallest, top_value):
    factor_of = 1.0
    for dim, blocks in cuts:
        heights = jax.random.uniform(jax.random.fold_in(jax.random.fold_in(key, 6), dim), (blocks,), jnp.float32, smallest / len(cuts), top_value / len(cuts))
        factor_of = factor_of * jnp.repeat(jnp.exp(heights), extent[dim] // blocks).reshape((-1,) + (1,) * (len(extent) - 1 - dim))
    return factor_of


def profile(count, total, most, skew):
    loads = [(1 << 20) // math.isqrt(rank ** skew) + 1 for rank in range(2, count + 1)]
    rest, given = total - most - (count - 1), [1] * (count - 1)
    while rest > 0:
        free = [i for i in range(count - 1) if given[i] < most]
        mass, left = sum([loads[i] for i in free]), rest
        for i in free:
            more = min(most - given[i], max(1, left * loads[i] // mass), rest)
            given[i] = given[i] + more
            rest = rest - more
    return np.array([most] + given)


def uneven_parts(stream_key, amount, total, most, lean):
    if amount == 2:
        one = jax.random.randint(stream_key, (), max(1, total - most), min(most, total - 1) + 1)
        return jnp.stack([one, total - one])
    lengths = jnp.asarray(profile(amount, total, most, lean), jnp.int32)
    couples = (amount - 1) // 2
    source_of, sink = lengths[1:1 + 2 * couples:2], lengths[2:2 + 2 * couples:2]
    room = jnp.minimum(source_of - 1, most - sink)
    passed = jax.random.randint(jax.random.fold_in(stream_key, 1), (couples,), 0, 1 << 20) % (room + 1)
    lengths = lengths.at[1:1 + 2 * couples:2].set(source_of - passed).at[2:2 + 2 * couples:2].set(sink + passed)
    return lengths[jax.random.permutation(jax.random.fold_in(stream_key, 2), amount)]


def scatter_about(rng, shape, deviation, limit, cuts=(), kind=jnp.bfloat16):
    drawn = deviation * jax.random.normal(rng, shape, jnp.float32)
    if cuts:
        drawn = drawn * steps_of(rng, shape, cuts, -0.22, 0.18)
    return jnp.clip(drawn, -limit, limit).astype(kind)


def noise_with(key, extent, spread, bound, cuts, heavy, kind=jnp.bfloat16):
    entries = spread * jax.random.normal(key, extent, jnp.float32)
    if cuts:
        entries = entries * steps_of(key, extent, cuts, -0.22, 0.18)
    return jnp.clip(spiked(entries, jax.random.fold_in(key, 3), *heavy), -bound, bound).astype(kind)


def setup_inputs(seed: int = 0, part: int = 0) -> dict:
    key_list = jax.random.split(jax.random.key(seed), 7)
    part_splits = jax.random.split(jax.random.fold_in(key_list[6], part), 7)
    output_gradient = noise_with(part_splits[0], (TOKENS, OUTPUT_FEATURES), 1.0, 6.0, ((0, 4), (1, 4)), (1, 0, 4, 2.0))
    hidden_input = scatter_about(part_splits[1], (TOKENS, HIDDEN_UNITS), 1.0, 6.0, ((0, 4), (1, 4)))
    frozen_down_matrix = scatter_about(key_list[2], (HIDDEN_UNITS, OUTPUT_FEATURES), OUTPUT_FEATURES ** -0.5, 0.0625, ((0, 4), (1, 4)))
    down_factors = scatter_about(part_splits[3], (ADAPTER_SLOTS, ADAPTER_RANK, HIDDEN_UNITS), HIDDEN_UNITS ** -0.5, 0.03125, ((2, 4),))
    up_factors = scatter_about(part_splits[4], (ADAPTER_SLOTS, ADAPTER_RANK, OUTPUT_FEATURES), (2.0 / OUTPUT_FEATURES ** 0.5), 0.13183594, ((2, 4),))
    token_adapter_index = jnp.searchsorted(jnp.cumsum(uneven_parts(part_splits[5], ADAPTER_SLOTS, TOKENS, TOKENS // 2, 2)), jnp.arange(TOKENS), side="right").astype(jnp.int32)
    return dict(output_gradient=output_gradient, hidden_input=hidden_input, frozen_down_matrix=frozen_down_matrix, down_factors=down_factors, up_factors=up_factors, token_adapter_index=token_adapter_index)


ADAPTER_SCALE = 4.0


def reference(output_gradient, hidden_input, frozen_down_matrix, down_factors, up_factors, token_adapter_index):
    shards = N_DP * N_SUB
    block = OUTPUT_FEATURES // shards
    frozen_term = jnp.zeros((TOKENS, HIDDEN_UNITS), jnp.float32)
    for index in range(shards):
        piece = jnp.dot(output_gradient[:, index * block:(index + 1) * block],
                        frozen_down_matrix[:, index * block:(index + 1) * block].T,
                        preferred_element_type=jnp.float32)
        rounded = lax.optimization_barrier(piece.astype(jnp.bfloat16))
        frozen_term = frozen_term + rounded.astype(jnp.float32)
    labels = jnp.arange(ADAPTER_SLOTS, dtype=jnp.int32)
    member = (token_adapter_index[:, None] == labels[None, :]).astype(jnp.float32)
    mask_cols = jnp.repeat(member, ADAPTER_RANK, axis=1)
    down_factor_flat = down_factors.reshape(ADAPTER_SLOTS * ADAPTER_RANK, HIDDEN_UNITS)
    up_factor_flat = up_factors.reshape(ADAPTER_SLOTS * ADAPTER_RANK, OUTPUT_FEATURES)
    rank_activation = (mask_cols * jnp.dot(output_gradient, up_factor_flat.T, preferred_element_type=jnp.float32)).astype(jnp.bfloat16)
    hidden_input_gradient = (frozen_term + ADAPTER_SCALE * jnp.dot(rank_activation, down_factor_flat, preferred_element_type=jnp.float32)).astype(jnp.bfloat16)
    down_factor_gradient = (ADAPTER_SCALE / SHARD_TOKENS) * jnp.dot(rank_activation.T, hidden_input, preferred_element_type=jnp.float32)
    down_rank_product = (mask_cols * jnp.dot(hidden_input, down_factor_flat.T, preferred_element_type=jnp.float32)).astype(jnp.bfloat16)
    up_factor_gradient = (ADAPTER_SCALE / SHARD_TOKENS) * jnp.dot(down_rank_product.T, output_gradient, preferred_element_type=jnp.float32)
    return hidden_input_gradient, down_factor_gradient.reshape(ADAPTER_SLOTS, ADAPTER_RANK, HIDDEN_UNITS), up_factor_gradient.reshape(ADAPTER_SLOTS, ADAPTER_RANK, OUTPUT_FEATURES)
```

```python
import functools

import jax
import jax.numpy as jnp
from jax import lax
from jax.experimental import pallas as pl
from jax.experimental.pallas import tpu as pltpu
from jax.sharding import PartitionSpec as P

ADAPTER_SCALE = 4.0
CHUNK = 512
MESH = pl.DeviceIdType.MESH


def contract(left, right, left_dim, right_dim):
    return lax.dot_general(
        left, right, (((left_dim,), (right_dim,)), ((), ())), preferred_element_type=jnp.float32
    )


def on_device_general(
    output_gradient, hidden_input, frozen_down_matrix, down_factors, up_factors, token_adapter_index
):
    adapter_total = down_factors.shape[0]
    rank_span = down_factors.shape[1]
    down_factor_flat = down_factors.reshape(adapter_total * rank_span, down_factors.shape[2])
    up_factor_flat = up_factors.reshape(adapter_total * rank_span, up_factors.shape[2])
    local_rows = hidden_input.shape[0]
    panels_all = lax.all_gather(output_gradient, "tensor", axis=0, tiled=True)
    frozen_term = lax.psum_scatter(
        contract(panels_all, frozen_down_matrix, 1, 1).astype(jnp.bfloat16),
        ("dp", "sub"),
        scatter_dimension=0,
        tiled=True,
    ).astype(jnp.float32)
    labels = jnp.arange(adapter_total, dtype=jnp.int32)
    member = (token_adapter_index[:, None] == labels[None, :]).astype(jnp.float32)
    mask_cols = jnp.repeat(member, rank_span, axis=1)
    low_part = contract(panels_all, up_factor_flat, 1, 1)
    low_rows = lax.psum_scatter(
        low_part.astype(jnp.bfloat16), ("dp", "sub"), scatter_dimension=0, tiled=True
    ).astype(jnp.float32)
    rank_activation = (mask_cols * low_rows).astype(jnp.bfloat16)
    hidden_input_gradient = (
        frozen_term
        + ADAPTER_SCALE
        * jnp.dot(rank_activation, down_factor_flat, preferred_element_type=jnp.float32)
    ).astype(jnp.bfloat16)
    scale_factor = ADAPTER_SCALE / local_rows
    a_part = scale_factor * contract(rank_activation, hidden_input, 0, 0)
    down_factor_gradient = (
        lax.psum(a_part.astype(jnp.bfloat16), ("dp", "sub"))
        .astype(jnp.float32)
        .reshape(adapter_total, rank_span, -1)
    )
    down_part = contract(hidden_input, down_factor_flat, 1, 1)
    down_full = lax.psum(down_part.astype(jnp.bfloat16), "tensor").astype(jnp.float32)
    down_rank_product = (mask_cols * down_full).astype(jnp.bfloat16)
    down_every = lax.all_gather(down_rank_product, ("dp", "sub"), axis=0, tiled=True)
    slab_rows = output_gradient.shape[0]
    first_slab = lax.axis_index("tensor") * slab_rows
    down_mine = lax.dynamic_slice_in_dim(down_every, first_slab, slab_rows, 0)
    b_total = lax.psum(
        (scale_factor * contract(down_mine, output_gradient, 0, 0)).astype(jnp.bfloat16), "tensor"
    ).astype(jnp.float32)
    up_factor_gradient = b_total.reshape(adapter_total, rank_span, -1)
    return (hidden_input_gradient, down_factor_gradient, up_factor_gradient)


def kernel(
    scale, og, h, w, a, b, mask, dh_out, da_out, db_out,
    panels, bv, hv, av, wv, acc, own_l, sib_l, out_c, sib_c, out_x, in_x, in_a, sum_a, dbv,
    low_p, low_in, low, dn_p, dn_t,
    load, wload, g_send, g_recv, lp_send, lp_recv, lo_send, lo_recv, dn_send, dn_recv,
    dt_send, dt_recv, l_send, l_recv, c_send, c_recv, x_send, x_recv, a_recv,
    d_copy, d_send, d_recv, h_copy, b_copy,
):
    g, z = lax.axis_index("groups"), lax.axis_index("tensor")
    x, c = lax.axis_index("dp"), lax.axis_index("sub")
    d = 2 * x + c
    n_chunks = wv.shape[0]
    half = n_chunks // 2
    sibling = (g, z, x, 1 - c)
    across = (g, z, 1 - x, c)
    plane = (sibling, across, (g, z, 1 - x, 1 - c))
    line = tuple((g, (z + k) % 4, x, c) for k in (1, 2, 3))

    def send(src, dst, send_sem, recv_sem, device):
        return pltpu.make_async_remote_copy(
            src_ref=src, dst_ref=dst, send_sem=send_sem, recv_sem=recv_sem,
            device_id=device, device_id_type=MESH,
        )

    def arrived(dst, recv_sem):
        send(dst, dst, l_send.at[0], recv_sem, sibling).wait_recv()

    def sent(src, send_sem):
        send(src, src, send_sem, l_recv.at[0], sibling).wait_send()

    loads = [
        pltpu.make_async_copy(src, dst, load.at[k])
        for k, (src, dst) in enumerate(((og, panels.at[z]), (b, bv), (h, hv), (a, av)))
    ]
    for copy in loads:
        copy.start()

    def w_copy(j):
        return pltpu.make_async_copy(w.at[pl.ds(j * CHUNK, CHUNK)], wv.at[j], wload.at[j])

    def column_chunk(t):
        side = (t // half + 1 + c) % 2
        return side * half + t % half

    @pl.loop(0, n_chunks)
    def _(t):
        w_copy(column_chunk(t)).start()

    barrier = pltpu.get_barrier_semaphore()
    for peer in plane + line:
        pl.semaphore_signal(barrier, inc=1, device_id=peer, device_id_type=MESH)
    pl.semaphore_wait(barrier, 6)

    def own_left():
        return send(og, panels.at[z], g_send.at[0], g_recv.at[z], (g, z - 1, x, c))

    def own_right():
        return send(og, panels.at[z], g_send.at[1], g_recv.at[z], (g, z + 1, x, c))

    @pl.when(z > 0)
    def _():
        own_left().start()

    @pl.when(z < 3)
    def _():
        own_right().start()

    loads[0].wait()
    loads[1].wait()
    low_p[...] = contract(panels[z], bv[...], 1, 1).astype(jnp.bfloat16)

    @pl.when(d != z)
    def _():
        send(low_p, low_in.at[d], lp_send, lp_recv.at[d], (g, z, z // 2, z % 2)).start()

    loads[2].wait()
    loads[3].wait()

    def down_step(j, total):
        cols = pl.ds(pl.multiple_of(j * CHUNK, CHUNK), CHUNK)
        return total + contract(hv[:, cols], av[:, cols], 1, 1)

    rank_rows = (mask.shape[0], mask.shape[1])
    dn_p[z] = lax.fori_loop(0, n_chunks, down_step, jnp.zeros(rank_rows, jnp.float32)).astype(
        jnp.bfloat16
    )
    for k, peer in enumerate(line):
        send(dn_p.at[z], dn_p.at[z], dn_send.at[k], dn_recv.at[z], peer).start()

    @pl.when(d == z)
    def _():
        total = low_p[...].astype(jnp.float32)
        for k in (1, 2, 3):
            other = (d + k) % 4
            arrived(low_in.at[other], lp_recv.at[other])
            total = total + low_in[other].astype(jnp.float32)
        low[...] = (mask[...] * total).astype(jnp.bfloat16)
        for k, peer in enumerate(line):
            send(low, low, lo_send.at[k], lo_recv, peer).start()

    @pl.when(d != z)
    def _():
        arrived(low, lo_recv)

    def give_sibling(k, t, value):
        out_c[k, t] = value.astype(jnp.bfloat16)
        send(out_c.at[k, t], sib_c.at[k, t], c_send.at[k, t], c_recv.at[k, t], sibling).start()

    def add_sibling(k, t, value):
        arrived(sib_c.at[k, t], c_recv.at[k, t])
        out_x[k, t] = (value + sib_c[k, t].astype(jnp.float32)).astype(jnp.bfloat16)

    low_t = low[...].astype(jnp.float32).T.astype(jnp.bfloat16)

    def a_part(t):
        cols = pl.ds(pl.multiple_of(column_chunk(t) * CHUNK, CHUNK), CHUNK)
        return scale * jnp.dot(low_t, hv[:, cols], preferred_element_type=jnp.float32)

    @pl.loop(0, half)
    def _(t):
        give_sibling(2, t, a_part(t))

    @pl.loop(0, half)
    def _(t):
        add_sibling(2, t, a_part(t + half))
        send(out_x.at[2, t], in_a.at[t], x_send.at[2, t], a_recv.at[t], across).start()

    def forward(block):
        @pl.when((block < z) & (z < 3))
        def _():
            send(
                panels.at[block], panels.at[block], g_send.at[2 + block], g_recv.at[block],
                (g, z + 1, x, c),
            ).start()

        @pl.when((block > z) & (z > 0))
        def _():
            send(
                panels.at[block], panels.at[block], g_send.at[2 + block], g_recv.at[block],
                (g, z - 1, x, c),
            ).start()

    def step(block, first):
        k = block % 2
        here = block // 2 == x

        def product(j):
            return contract(panels[block], wv[j], 1, 1)

        @pl.loop(0, half)
        def _(t):
            j = column_chunk(t)
            if first:
                w_copy(j).wait()
            value = product(j)

            @pl.when(here & (k == c))
            def _():
                acc[j] = value.astype(jnp.bfloat16)

            @pl.when(here & (k != c))
            def _():
                own_l[j] = value.astype(jnp.bfloat16)
                send(own_l.at[j], sib_l.at[j], l_send.at[j], l_recv.at[j], sibling).start()

            @pl.when(block // 2 != x)
            def _():
                give_sibling(k, t, value)

        @pl.loop(0, half)
        def _(t):
            j = column_chunk(t + half)
            if first:
                w_copy(j).wait()
            value = product(j)

            @pl.when(here & (k == c))
            def _():
                acc[j] = value.astype(jnp.bfloat16)

            @pl.when(here & (k != c))
            def _():
                own_l[j] = value.astype(jnp.bfloat16)
                send(own_l.at[j], sib_l.at[j], l_send.at[j], l_recv.at[j], sibling).start()

            @pl.when(block // 2 != x)
            def _():
                add_sibling(k, t, value)
                send(
                    out_x.at[k, t], in_x.at[j], x_send.at[k, t], x_recv.at[j], (g, z, 1 - x, k)
                ).start()

    end = 1 - (z % 3 + 1) // 2
    mids = (z, z + 1 - 2 * x, z - 1 + 2 * x, 3 * (2 - z))
    order = [end * (i + (z // 3) * (3 - 2 * i)) + (1 - end) * mids[i] for i in range(4)]

    step(order[0], True)
    arrived(panels.at[order[1]], g_recv.at[order[1]])
    forward(order[1])

    @pl.when(end == 0)
    def _():
        arrived(panels.at[order[2]], g_recv.at[order[2]])
        forward(order[2])

    step(order[1], False)

    for k in (1, 2, 3):
        other = (z + k) % 4
        arrived(dn_p.at[other], dn_recv.at[other])
    down = jnp.zeros(rank_rows, jnp.float32)
    for k in range(4):
        down = down + dn_p[k].astype(jnp.float32)
    dn_t[d] = (mask[...] * down).T.astype(jnp.bfloat16)
    for k, peer in enumerate(plane):
        send(dn_t.at[d], dn_t.at[d], dt_send.at[k], dt_recv.at[d], peer).start()

    @pl.when(end == 1)
    def _():
        arrived(panels.at[order[2]], g_recv.at[order[2]])

    step(order[2], False)
    arrived(panels.at[order[3]], g_recv.at[order[3]])
    forward(order[3])
    step(order[3], False)

    for k in (1, 2, 3):
        other = (d + k) % 4
        arrived(dn_t.at[other], dt_recv.at[other])

    @pl.loop(0, dbv.shape[1] // CHUNK)
    def _(j):
        cols = pl.ds(pl.multiple_of(j * CHUNK, CHUNK), CHUNK)
        total = jnp.dot(dn_t[0], panels[0, :, cols], preferred_element_type=jnp.float32)
        for k in (1, 2, 3):
            total += jnp.dot(dn_t[k], panels[k, :, cols], preferred_element_type=jnp.float32)
        dbv[:, cols] = scale * total

    db_copy = pltpu.make_async_copy(dbv, db_out, b_copy)
    db_copy.start()

    def a_cols(t):
        return pl.ds(pl.multiple_of((c * half + t) * CHUNK, CHUNK), CHUNK)

    def a_copy(t):
        return pltpu.make_async_copy(sum_a.at[t], da_out.at[:, a_cols(t)], d_copy.at[t])

    def a_give(t):
        where = da_out.at[:, a_cols(t)]
        return send(sum_a.at[t], where, d_send.at[t], d_recv.at[t], sibling)

    @pl.loop(0, half)
    def _(t):
        arrived(in_a.at[t], a_recv.at[t])
        sum_a[t] = (out_x[2, t].astype(jnp.float32) + in_a[t].astype(jnp.float32)).astype(
            jnp.bfloat16
        )
        a_copy(t).start()
        a_give(t).start()

    def h_out(j):
        cols = pl.ds(pl.multiple_of(j * CHUNK, CHUNK), CHUNK)
        return pltpu.make_async_copy(acc.at[j], dh_out.at[:, cols], h_copy.at[j])

    @pl.loop(0, n_chunks)
    def _(t):
        j = (t % 2) * half + t // 2
        cols = pl.ds(pl.multiple_of(j * CHUNK, CHUNK), CHUNK)
        rank_term = jnp.dot(low[...], av[:, cols], preferred_element_type=jnp.float32)
        arrived(sib_l.at[j], l_recv.at[j])
        arrived(in_x.at[j], x_recv.at[j])
        total = acc[j].astype(jnp.float32) + sib_l[j].astype(jnp.float32)
        total = total + in_x[j].astype(jnp.float32) + ADAPTER_SCALE * rank_term
        acc[j] = total.astype(jnp.bfloat16)
        h_out(j).start()

    @pl.loop(0, n_chunks)
    def _(j):
        h_out(j).wait()
        sent(own_l.at[j], l_send.at[j])

    @pl.loop(0, half)
    def _(t):
        a_copy(t).wait()
        a_give(t).wait_send()
        other = pl.ds(pl.multiple_of(((1 - c) * half + t) * CHUNK, CHUNK), CHUNK)
        arrived(da_out.at[:, other], d_recv.at[t])
        for k in range(3):
            sent(out_c.at[k, t], c_send.at[k, t])
            sent(out_x.at[k, t], x_send.at[k, t])

    db_copy.wait()
    for k in range(3):
        sent(dn_p.at[z], dn_send.at[k])
        sent(dn_t.at[d], dt_send.at[k])

    @pl.when(d == z)
    def _():
        for k in range(3):
            sent(low, lo_send.at[k])

    @pl.when(d != z)
    def _():
        sent(low_p, lp_send)

    @pl.when(z > 0)
    def _():
        own_left().wait_send()

    @pl.when(z < 3)
    def _():
        own_right().wait_send()

    @pl.when(end == 0)
    def _():
        for k in (1, 2, 3):
            sent(panels.at[order[k]], g_send.at[2 + order[k]])


def on_device_small(
    output_gradient, hidden_input, frozen_down_matrix, down_factors, up_factors, token_adapter_index
):
    adapters, rank, hidden = down_factors.shape
    ranks = adapters * rank
    rows, features = output_gradient.shape
    n_chunks = hidden // CHUNK
    half = n_chunks // 2
    labels = jnp.arange(adapters, dtype=jnp.int32)
    member = (token_adapter_index[:, None] == labels[None, :]).astype(jnp.float32)
    mask_cols = jnp.repeat(member, rank, axis=1)
    bf16, f32 = jnp.bfloat16, jnp.float32
    dma = pltpu.SemaphoreType.DMA

    def vmem(*shape, dtype=bf16):
        return pltpu.VMEM(shape, dtype)

    flops = 2 * 4 * rows * features * hidden
    hidden_gradient, down_gradient, up_gradient = pl.pallas_call(
        functools.partial(kernel, ADAPTER_SCALE / rows),
        out_shape=(
            jax.ShapeDtypeStruct((rows, hidden), bf16),
            jax.ShapeDtypeStruct((ranks, hidden), bf16),
            jax.ShapeDtypeStruct((ranks, features), f32),
        ),
        in_specs=[pl.BlockSpec(memory_space=pl.ANY)] * 5
        + [pl.BlockSpec(memory_space=pltpu.VMEM)],
        out_specs=[pl.BlockSpec(memory_space=pl.ANY)] * 3,
        scratch_shapes=[
            vmem(4, rows, features),
            vmem(ranks, features),
            vmem(rows, hidden),
            vmem(ranks, hidden),
            vmem(n_chunks, CHUNK, features),
            vmem(n_chunks, rows, CHUNK),
            vmem(n_chunks, rows, CHUNK),
            vmem(n_chunks, rows, CHUNK),
            vmem(3, half, rows, CHUNK),
            vmem(3, half, rows, CHUNK),
            vmem(3, half, rows, CHUNK),
            vmem(n_chunks, rows, CHUNK),
            vmem(half, rows, CHUNK),
            vmem(half, rows, CHUNK),
            vmem(ranks, features, dtype=f32),
            vmem(rows, ranks),
            vmem(4, rows, ranks),
            vmem(rows, ranks),
            vmem(4, rows, ranks),
            vmem(4, ranks, rows),
            dma((4,)),
            dma((n_chunks,)),
            dma((6,)),
            dma((4,)),
            dma,
            dma((4,)),
            dma((3,)),
            dma,
            dma((3,)),
            dma((4,)),
            dma((3,)),
            dma((4,)),
            dma((n_chunks,)),
            dma((n_chunks,)),
            dma((3, half)),
            dma((3, half)),
            dma((3, half)),
            dma((n_chunks,)),
            dma((half,)),
            dma((half,)),
            dma((half,)),
            dma((half,)),
            dma((n_chunks,)),
            dma,
        ],
        compiler_params=pltpu.CompilerParams(
            collective_id=0, has_side_effects=True, vmem_limit_bytes=60 << 20
        ),
        cost_estimate=pl.CostEstimate(
            flops=flops, bytes_accessed=2 * features * hidden, transcendentals=0
        ),
    )(
        output_gradient,
        hidden_input,
        frozen_down_matrix,
        down_factors.reshape(ranks, hidden),
        up_factors.reshape(ranks, features),
        mask_cols,
    )
    return (
        hidden_gradient,
        down_gradient.astype(f32).reshape(adapters, rank, hidden),
        up_gradient.reshape(adapters, rank, features),
    )


def solution(mesh):
    sizes = tuple(mesh.shape[n] for n in ("tensor", "dp", "sub"))
    fits = sizes == (4, 2, 2)
    return jax.shard_map(
        on_device_small if fits else on_device_general,
        mesh=mesh,
        in_specs=(
            P(("groups", "tensor"), ("dp", "sub")),
            P(("groups", "dp", "sub"), "tensor"),
            P("tensor", ("dp", "sub")),
            P("groups", None, "tensor"),
            P("groups", None, ("dp", "sub")),
            P(("groups", "dp", "sub")),
        ),
        out_specs=(
            P(("groups", "dp", "sub"), "tensor"),
            P("groups", None, "tensor"),
            P("groups", None, ("dp", "sub")),
        ),
        check_vma=False,
    )
```

```python
import functools

import jax
import jax.numpy as jnp
from jax import lax
from jax.experimental import pallas as pl
from jax.experimental.pallas import tpu as pltpu
from jax.sharding import PartitionSpec as P

ADAPTER_SCALE = 4.0
CHUNK = 512
MESH = pl.DeviceIdType.MESH


def contract(left, right, left_dim, right_dim):
    return lax.dot_general(
        left, right, (((left_dim,), (right_dim,)), ((), ())), preferred_element_type=jnp.float32
    )


def on_device_general(
    output_gradient, hidden_input, frozen_down_matrix, down_factors, up_factors, token_adapter_index
):
    adapter_total = down_factors.shape[0]
    rank_span = down_factors.shape[1]
    down_factor_flat = down_factors.reshape(adapter_total * rank_span, down_factors.shape[2])
    up_factor_flat = up_factors.reshape(adapter_total * rank_span, up_factors.shape[2])
    local_rows = hidden_input.shape[0]
    panels_all = lax.all_gather(output_gradient, "tensor", axis=0, tiled=True)
    frozen_term = lax.psum_scatter(
        contract(panels_all, frozen_down_matrix, 1, 1).astype(jnp.bfloat16),
        ("dp", "sub"),
        scatter_dimension=0,
        tiled=True,
    ).astype(jnp.float32)
    labels = jnp.arange(adapter_total, dtype=jnp.int32)
    member = (token_adapter_index[:, None] == labels[None, :]).astype(jnp.float32)
    mask_cols = jnp.repeat(member, rank_span, axis=1)
    low_part = contract(panels_all, up_factor_flat, 1, 1)
    low_rows = lax.psum_scatter(
        low_part.astype(jnp.bfloat16), ("dp", "sub"), scatter_dimension=0, tiled=True
    ).astype(jnp.float32)
    rank_activation = (mask_cols * low_rows).astype(jnp.bfloat16)
    hidden_input_gradient = (
        frozen_term
        + ADAPTER_SCALE
        * jnp.dot(rank_activation, down_factor_flat, preferred_element_type=jnp.float32)
    ).astype(jnp.bfloat16)
    scale_factor = ADAPTER_SCALE / local_rows
    a_part = scale_factor * contract(rank_activation, hidden_input, 0, 0)
    down_factor_gradient = (
        lax.psum(a_part.astype(jnp.bfloat16), ("dp", "sub"))
        .astype(jnp.float32)
        .reshape(adapter_total, rank_span, -1)
    )
    down_part = contract(hidden_input, down_factor_flat, 1, 1)
    down_full = lax.psum(down_part.astype(jnp.bfloat16), "tensor").astype(jnp.float32)
    down_rank_product = (mask_cols * down_full).astype(jnp.bfloat16)
    down_every = lax.all_gather(down_rank_product, ("dp", "sub"), axis=0, tiled=True)
    slab_rows = output_gradient.shape[0]
    first_slab = lax.axis_index("tensor") * slab_rows
    down_mine = lax.dynamic_slice_in_dim(down_every, first_slab, slab_rows, 0)
    b_total = lax.psum(
        (scale_factor * contract(down_mine, output_gradient, 0, 0)).astype(jnp.bfloat16), "tensor"
    ).astype(jnp.float32)
    up_factor_gradient = b_total.reshape(adapter_total, rank_span, -1)
    return (hidden_input_gradient, down_factor_gradient, up_factor_gradient)


def kernel(
    scale, adapters, og, h, w, a, b, labels, dh_out, da_out, db_out,
    panels, bv, hv, av, wv, acc, own_l, sib_l, out_c, sib_c, out_x, in_x, in_a, sum_a, sib_a, dav, dbv,
    low_p, low_in, low_t, low, dn_p, dn_t,
    load, wload, g_send, g_recv, lp_send, lp_recv, lo_send, lo_recv, dn_send, dn_recv,
    dt_send, dt_recv, l_send, l_recv, c_send, c_recv, x_send, x_recv, a_recv,
    d_copy, d_send, d_recv, h_copy, b_copy,
):
    g, z = lax.axis_index("groups"), lax.axis_index("tensor")
    x, c = lax.axis_index("dp"), lax.axis_index("sub")
    d = 2 * x + c
    n_chunks = wv.shape[0]
    half = n_chunks // 2
    sibling = (g, z, x, 1 - c)
    across = (g, z, 1 - x, c)
    plane = (sibling, across, (g, z, 1 - x, 1 - c))
    line = tuple((g, (z + k) % 4, x, c) for k in (1, 2, 3))

    def send(src, dst, send_sem, recv_sem, device):
        return pltpu.make_async_remote_copy(
            src_ref=src, dst_ref=dst, send_sem=send_sem, recv_sem=recv_sem,
            device_id=device, device_id_type=MESH,
        )

    def arrived(dst, recv_sem):
        send(dst, dst, l_send.at[0], recv_sem, sibling).wait_recv()

    def sent(src, send_sem):
        send(src, src, send_sem, l_recv.at[0], sibling).wait_send()

    loads = [
        pltpu.make_async_copy(src, dst, load.at[k])
        for k, (src, dst) in enumerate(((og, panels.at[z]), (b, bv), (h, hv), (a, av)))
    ]
    for copy in loads:
        copy.start()

    def w_copy(j):
        return pltpu.make_async_copy(w.at[pl.ds(j * CHUNK, CHUNK)], wv.at[j], wload.at[j])

    def column_chunk(t):
        side = (t // half + 1 + c) % 2
        return side * half + t % half

    barrier = pltpu.get_barrier_semaphore()
    for peer in plane + line:
        pl.semaphore_signal(barrier, inc=1, device_id=peer, device_id_type=MESH)
    pl.semaphore_wait(barrier, 6)

    def own_left():
        return send(og, panels.at[z], g_send.at[0], g_recv.at[z], (g, z - 1, x, c))

    def own_right():
        return send(og, panels.at[z], g_send.at[1], g_recv.at[z], (g, z + 1, x, c))

    @pl.when(z > 0)
    def _():
        own_left().start()

    @pl.when(z < 3)
    def _():
        own_right().start()

    rank_rows = (low_t.shape[0], low_t.shape[1])
    rank_of_row = lax.broadcasted_iota(jnp.int32, rank_rows, 0) // (rank_rows[0] // adapters)
    mask = jnp.where(rank_of_row == labels[...], 1.0, 0.0)
    loads[0].wait()
    loads[1].wait()
    low_p[...] = contract(bv[...], panels[z], 1, 1).astype(jnp.bfloat16)

    @pl.when(d != z)
    def _():
        send(low_p, low_in.at[d], lp_send, lp_recv.at[d], (g, z, z // 2, z % 2)).start()

    loads[2].wait()
    loads[3].wait()

    @pl.loop(0, n_chunks)
    def _(t):
        w_copy(column_chunk(t)).start()

    @pl.when(d == z)
    def _():
        total = low_p[...].astype(jnp.float32)
        for k in (1, 2, 3):
            other = (d + k) % 4
            arrived(low_in.at[other], lp_recv.at[other])
            total = total + low_in[other].astype(jnp.float32)
        low_t[...] = (mask * total).astype(jnp.bfloat16)
        for k, peer in enumerate(line):
            send(low_t, low_t, lo_send.at[k], lo_recv, peer).start()

    @pl.when(d != z)
    def _():
        arrived(low_t, lo_recv)

    def give_sibling(k, t, value):
        out_c[k, t] = value.astype(jnp.bfloat16)
        send(out_c.at[k, t], sib_c.at[k, t], c_send.at[k, t], c_recv.at[k, t], sibling).start()

    def add_sibling(k, t, value):
        arrived(sib_c.at[k, t], c_recv.at[k, t])
        out_x[k, t] = (value + sib_c[k, t].astype(jnp.float32)).astype(jnp.bfloat16)

    def a_part(t):
        cols = pl.ds(pl.multiple_of(column_chunk(t) * CHUNK, CHUNK), CHUNK)
        return scale * jnp.dot(low_t[...], hv[:, cols], preferred_element_type=jnp.float32)

    @pl.loop(0, half)
    def _(t):
        give_sibling(2, t, a_part(t))

    @pl.loop(0, half)
    def _(t):
        add_sibling(2, t, a_part(t + half))
        send(out_x.at[2, t], in_a.at[t], x_send.at[2, t], a_recv.at[t], across).start()

    low[...] = low_t[...].astype(jnp.float32).T.astype(jnp.bfloat16)

    def down_step(j, total):
        cols = pl.ds(pl.multiple_of(j * CHUNK, CHUNK), CHUNK)
        return total + contract(av[:, cols], hv[:, cols], 1, 1)

    dn_p[z] = lax.fori_loop(0, n_chunks, down_step, jnp.zeros(rank_rows, jnp.float32)).astype(
        jnp.bfloat16
    )
    for k, peer in enumerate(line):
        send(dn_p.at[z], dn_p.at[z], dn_send.at[k], dn_recv.at[z], peer).start()

    def forward(block):
        @pl.when((block < z) & (z < 3))
        def _():
            send(
                panels.at[block], panels.at[block], g_send.at[2 + block], g_recv.at[block],
                (g, z + 1, x, c),
            ).start()

        @pl.when((block > z) & (z > 0))
        def _():
            send(
                panels.at[block], panels.at[block], g_send.at[2 + block], g_recv.at[block],
                (g, z - 1, x, c),
            ).start()

    def step(block, first, between=None):
        k = block % 2
        here = block // 2 == x

        def product(j):
            return contract(panels[block], wv[j], 1, 1)

        @pl.loop(0, half)
        def _(t):
            j = column_chunk(t)
            if first:
                w_copy(j).wait()
            value = product(j)

            @pl.when(here & (k == c))
            def _():
                acc[j] = value.astype(jnp.bfloat16)

            @pl.when(here & (k != c))
            def _():
                own_l[j] = value.astype(jnp.bfloat16)
                send(own_l.at[j], sib_l.at[j], l_send.at[j], l_recv.at[j], sibling).start()

            @pl.when(block // 2 != x)
            def _():
                give_sibling(k, t, value)

        if between is not None:
            between()

        @pl.loop(0, half)
        def _(t):
            j = column_chunk(t + half)
            if first:
                w_copy(j).wait()
            value = product(j)

            @pl.when(here & (k == c))
            def _():
                acc[j] = value.astype(jnp.bfloat16)

            @pl.when(here & (k != c))
            def _():
                own_l[j] = value.astype(jnp.bfloat16)
                send(own_l.at[j], sib_l.at[j], l_send.at[j], l_recv.at[j], sibling).start()

            @pl.when(block // 2 != x)
            def _():
                add_sibling(k, t, value)
                send(
                    out_x.at[k, t], in_x.at[j], x_send.at[k, t], x_recv.at[j], (g, z, 1 - x, k)
                ).start()

    end = 1 - (z % 3 + 1) // 2
    mids = (z, z + 1 - 2 * x, z - 1 + 2 * x, 3 * (2 - z))
    order = [end * (i + (z // 3) * (3 - 2 * i)) + (1 - end) * mids[i] for i in range(4)]

    def take(block):
        arrived(panels.at[block], g_recv.at[block])
        forward(block)

    @pl.when(end == 0)
    def _():
        take(order[1])
        take(order[2])

    step(order[0], True)

    for k in (1, 2, 3):
        other = (z + k) % 4
        arrived(dn_p.at[other], dn_recv.at[other])
    down = jnp.zeros(rank_rows, jnp.float32)
    for k in range(4):
        down = down + dn_p[k].astype(jnp.float32)
    dn_t[d] = (mask * down).astype(jnp.bfloat16)
    for k, peer in enumerate(plane):
        send(dn_t.at[d], dn_t.at[d], dt_send.at[k], dt_recv.at[d], peer).start()

    @pl.when(end == 1)
    def _():
        take(order[1])

    def take_last():
        @pl.when(end == 0)
        def _():
            take(order[3])

    step(order[1], False, take_last)

    @pl.when(end == 1)
    def _():
        take(order[2])

    step(order[2], False)

    def a_copy(j):
        cols = pl.ds(pl.multiple_of(j * CHUNK, CHUNK), CHUNK)
        return pltpu.make_async_copy(dav.at[j], da_out.at[:, cols], d_copy.at[j])

    def a_give(t):
        return send(sum_a.at[t], sib_a.at[t], d_send.at[t], d_recv.at[t], sibling)

    @pl.loop(0, half)
    def _(t):
        arrived(in_a.at[t], a_recv.at[t])
        total = out_x[2, t].astype(jnp.float32) + in_a[t].astype(jnp.float32)
        sum_a[t] = total.astype(jnp.bfloat16)
        a_give(t).start()
        dav[c * half + t] = sum_a[t].astype(jnp.float32)
        a_copy(c * half + t).start()

    @pl.when(end == 1)
    def _():
        take(order[3])

    step(order[3], False)

    @pl.loop(0, half)
    def _(t):
        arrived(sib_a.at[t], d_recv.at[t])
        dav[(1 - c) * half + t] = sib_a[t].astype(jnp.float32)
        a_copy((1 - c) * half + t).start()

    for k in (1, 2, 3):
        other = (d + k) % 4
        arrived(dn_t.at[other], dt_recv.at[other])

    @pl.loop(0, dbv.shape[1] // CHUNK)
    def _(j):
        cols = pl.ds(pl.multiple_of(j * CHUNK, CHUNK), CHUNK)
        total = jnp.dot(dn_t[0], panels[0, :, cols], preferred_element_type=jnp.float32)
        for k in (1, 2, 3):
            total += jnp.dot(dn_t[k], panels[k, :, cols], preferred_element_type=jnp.float32)
        dbv[:, cols] = scale * total

    db_copy = pltpu.make_async_copy(dbv, db_out, b_copy)
    db_copy.start()

    def h_out(j):
        cols = pl.ds(pl.multiple_of(j * CHUNK, CHUNK), CHUNK)
        return pltpu.make_async_copy(acc.at[j], dh_out.at[:, cols], h_copy.at[j])

    @pl.loop(0, n_chunks)
    def _(t):
        j = (t % 2) * half + t // 2
        cols = pl.ds(pl.multiple_of(j * CHUNK, CHUNK), CHUNK)
        rank_term = jnp.dot(low[...], av[:, cols], preferred_element_type=jnp.float32)
        arrived(sib_l.at[j], l_recv.at[j])
        arrived(in_x.at[j], x_recv.at[j])
        total = acc[j].astype(jnp.float32) + sib_l[j].astype(jnp.float32)
        total = total + in_x[j].astype(jnp.float32) + ADAPTER_SCALE * rank_term
        acc[j] = total.astype(jnp.bfloat16)
        h_out(j).start()

    @pl.loop(0, n_chunks)
    def _(j):
        h_out(j).wait()
        sent(own_l.at[j], l_send.at[j])

    @pl.loop(0, half)
    def _(t):
        a_copy(t).wait()
        a_copy(half + t).wait()
        a_give(t).wait_send()
        for k in range(3):
            sent(out_c.at[k, t], c_send.at[k, t])
            sent(out_x.at[k, t], x_send.at[k, t])

    db_copy.wait()
    for k in range(3):
        sent(dn_p.at[z], dn_send.at[k])
        sent(dn_t.at[d], dt_send.at[k])

    @pl.when(d == z)
    def _():
        for k in range(3):
            sent(low_t, lo_send.at[k])

    @pl.when(d != z)
    def _():
        sent(low_p, lp_send)

    @pl.when(z > 0)
    def _():
        own_left().wait_send()

    @pl.when(z < 3)
    def _():
        own_right().wait_send()

    @pl.when(end == 0)
    def _():
        for k in (1, 2, 3):
            sent(panels.at[order[k]], g_send.at[2 + order[k]])


def on_device_small(
    output_gradient, hidden_input, frozen_down_matrix, down_factors, up_factors, token_adapter_index
):
    adapters, rank, hidden = down_factors.shape
    ranks = adapters * rank
    rows, features = output_gradient.shape
    n_chunks = hidden // CHUNK
    half = n_chunks // 2
    bf16, f32 = jnp.bfloat16, jnp.float32
    dma = pltpu.SemaphoreType.DMA

    def vmem(*shape, dtype=bf16):
        return pltpu.VMEM(shape, dtype)

    flops = 2 * 4 * rows * features * hidden
    hidden_gradient, down_gradient, up_gradient = pl.pallas_call(
        functools.partial(kernel, ADAPTER_SCALE / rows, adapters),
        out_shape=(
            jax.ShapeDtypeStruct((rows, hidden), bf16),
            jax.ShapeDtypeStruct((ranks, hidden), f32),
            jax.ShapeDtypeStruct((ranks, features), f32),
        ),
        in_specs=[pl.BlockSpec(memory_space=pl.ANY)] * 5
        + [pl.BlockSpec(memory_space=pltpu.VMEM)],
        out_specs=[pl.BlockSpec(memory_space=pl.ANY)] * 3,
        scratch_shapes=[
            vmem(4, rows, features),
            vmem(ranks, features),
            vmem(rows, hidden),
            vmem(ranks, hidden),
            vmem(n_chunks, CHUNK, features),
            vmem(n_chunks, rows, CHUNK),
            vmem(n_chunks, rows, CHUNK),
            vmem(n_chunks, rows, CHUNK),
            vmem(3, half, rows, CHUNK),
            vmem(3, half, rows, CHUNK),
            vmem(3, half, rows, CHUNK),
            vmem(n_chunks, rows, CHUNK),
            vmem(half, rows, CHUNK),
            vmem(half, rows, CHUNK),
            vmem(half, rows, CHUNK),
            vmem(n_chunks, rows, CHUNK, dtype=f32),
            vmem(ranks, features, dtype=f32),
            vmem(ranks, rows),
            vmem(4, ranks, rows),
            vmem(ranks, rows),
            vmem(rows, ranks),
            vmem(4, ranks, rows),
            vmem(4, ranks, rows),
            dma((4,)),
            dma((n_chunks,)),
            dma((6,)),
            dma((4,)),
            dma,
            dma((4,)),
            dma((3,)),
            dma,
            dma((3,)),
            dma((4,)),
            dma((3,)),
            dma((4,)),
            dma((n_chunks,)),
            dma((n_chunks,)),
            dma((3, half)),
            dma((3, half)),
            dma((3, half)),
            dma((n_chunks,)),
            dma((half,)),
            dma((n_chunks,)),
            dma((half,)),
            dma((half,)),
            dma((n_chunks,)),
            dma,
        ],
        compiler_params=pltpu.CompilerParams(
            collective_id=0, has_side_effects=True, vmem_limit_bytes=60 << 20
        ),
        cost_estimate=pl.CostEstimate(
            flops=flops, bytes_accessed=2 * features * hidden, transcendentals=0
        ),
    )(
        output_gradient,
        hidden_input,
        frozen_down_matrix,
        down_factors.reshape(ranks, hidden),
        up_factors.reshape(ranks, features),
        token_adapter_index.reshape(1, rows),
    )
    return (
        hidden_gradient,
        down_gradient.reshape(adapters, rank, hidden),
        up_gradient.reshape(adapters, rank, features),
    )


def solution(mesh):
    sizes = tuple(mesh.shape[n] for n in ("tensor", "dp", "sub"))
    fits = sizes == (4, 2, 2)
    return jax.shard_map(
        on_device_small if fits else on_device_general,
        mesh=mesh,
        in_specs=(
            P(("groups", "tensor"), ("dp", "sub")),
            P(("groups", "dp", "sub"), "tensor"),
            P("tensor", ("dp", "sub")),
            P("groups", None, "tensor"),
            P("groups", None, ("dp", "sub")),
            P(("groups", "dp", "sub")),
        ),
        out_specs=(
            P(("groups", "dp", "sub"), "tensor"),
            P("groups", None, "tensor"),
            P("groups", None, ("dp", "sub")),
        ),
        check_vma=False,
    )
```
